512 devices in a mesh: replica: 8 (over y_hi, core), fsdp: 8 (over x, y_lo), tensor: 8 (over z).
Axes of the slice: x: 4, y: 8 (y_hi: 4, y_lo: 2; y = y_hi * 2 + y_lo), z: 8, core: 2. Of those that a mesh axis runs over, the one named last changes fastest.
Arguments:
- grad_parts: bfloat16 [8, 8, 512, 8192], P('replica', 'fsdp', 'tensor'), may hold values from -12 to 12
- inner_params: float32 [8, 512, 8192], P('replica', 'tensor', 'fsdp'), may hold values from -0.12 to 0.12
- first_moment: float32 [8, 512, 8192], P('replica', 'tensor', 'fsdp'), may hold values from -4 to 4
- second_moment: float32 [8, 512, 8192], P('replica', 'tensor', 'fsdp'), may hold values from 0.1 to 10
- outer_params: float32 [8, 512, 1024], P('replica', 'tensor', 'fsdp'), may hold values from -0.12 to 0.12
- outer_momentum: float32 [8, 512, 1024], P('replica', 'tensor', 'fsdp'), may hold values from -0.06 to 0.06
Outputs:
- next_weights: float32 [512, 8192], P('tensor')
- outer_params_out: float32 [8, 512, 1024], P('replica', 'tensor', 'fsdp')
- outer_momentum_out: float32 [8, 512, 1024], P('replica', 'tensor', 'fsdp')
- first_out: float32 [8, 512, 8192], P('replica', 'tensor', 'fsdp')
- second_out: float32 [8, 512, 8192], P('replica', 'tensor', 'fsdp')
The draws below stay inside these ranges and needn't reach their ends.
All inputs are finite; a program needn't handle non-finite values.
Results may differ from the reference program's by a relative error of at most 0.0003.
Values may be sent and summed in bfloat16 or wider, within the bound.
A program may use at most 64 MiB of HBM per device.

```python
import math
import jax
import jax.numpy as jnp
from jax import lax

D = 8192
STEP = 100
KVW = 512
REPLICAS = 8
SHARE = 128
OUTER_COLS = 1024
N_REPLICA = 8
N_FSDP = 8


def draw_grad_parts(key, part):
    key_rows, key_cols, key_common, key_private = jax.random.split(key, 4)
    row_scale = jnp.exp(jax.random.uniform(key_rows, (KVW, 1), jnp.float32, math.log(0.5), math.log(2.0)))
    col_scale = jnp.exp(jax.random.uniform(key_cols, (1, D), jnp.float32, math.log(0.5), math.log(2.0)))
    common = jax.random.normal(key_common, (KVW, D), jnp.float32) * row_scale * col_scale
    private = jax.random.normal(key_private, (REPLICAS, N_FSDP, KVW, D), jnp.float32)
    values = jnp.clip(common[None, None] + private, -12.0, 12.0)
    return values.astype(jnp.bfloat16)


def level_of(rng, shape, cuts, low, largest):
    loudness, own = 1.0, jax.random.fold_in(rng, 6)
    for position, shards_of in cuts:
        heights = jnp.exp(jax.random.uniform(jax.random.fold_in(own, position), (shards_of,), jnp.float32, low / len(cuts), largest / len(cuts)))
        loudness = loudness * jnp.repeat(heights, shape[position] // shards_of).reshape([-1 if axis == position else 1 for axis in range(len(shape))])
    return loudness


def scatter_about(stream_key, dims, spread, most, cuts=(), dtype=jnp.bfloat16):
    entries = spread * jax.random.normal(stream_key, dims, jnp.float32)
    if cuts:
        entries = entries * level_of(stream_key, dims, cuts, -0.22, 0.18)
    return jnp.clip(entries, -most, most).astype(dtype)


def setup_inputs(seed: int = 0) -> dict:
    key_of = jax.random.split(jax.random.key(seed), 7)
    grad_parts = draw_grad_parts(jax.random.fold_in(key_of[6], 71), 0)
    inner_params = scatter_about(key_of[1], (REPLICAS, KVW, D), 0.02, 0.12, ((0, 8), (1, 8), (2, 8)), jnp.float32)
    first_moment = scatter_about(key_of[2], (REPLICAS, KVW, D), 0.5, 4.0, ((0, 8), (1, 8), (2, 8)), jnp.float32)
    second_moment = jnp.clip(jnp.exp(math.log(10.0) - 4.6051702 * jax.random.uniform(key_of[3], (REPLICAS, KVW, D), jnp.float32) ** level_of(key_of[3], (REPLICAS, KVW, D), ((0, 8), (1, 8), (2, 8)), -0.2, 0.2)), 0.1, 10.0)
    outer_params = scatter_about(key_of[4], (REPLICAS, KVW, OUTER_COLS), 0.02, 0.12, ((0, 8), (1, 8), (2, 8)), jnp.float32)
    outer_momentum = scatter_about(key_of[5], (REPLICAS, KVW, OUTER_COLS), 0.01, 0.06, ((0, 8), (1, 8), (2, 8)), jnp.float32)
    return dict(grad_parts=grad_parts, inner_params=inner_params, first_moment=first_moment, second_moment=second_moment, outer_params=outer_params, outer_momentum=outer_momentum)


beta_first = 0.9
beta_second = 0.95
inner_rate = 0.01
weight_decay = 0.1
epsilon = 1e-08
outer_rate = 0.7
momentum_factor = 0.9

def inner_adamw(gradient, params, first_in, second_in):
    first_out = beta_first * first_in + (1.0 - beta_first) * gradient
    second_out = beta_second * second_in + (1.0 - beta_second) * gradient * gradient
    first_scale = 1.0 / (1.0 - beta_first ** STEP)
    second_scale = 1.0 / (1.0 - beta_second ** STEP)
    direction = first_out * first_scale / (jnp.sqrt(second_out * second_scale) + epsilon)
    updated = params - inner_rate * (direction + weight_decay * params)
    return (first_out, second_out, updated)

def nesterov(mean_params, outer_in, momentum):
    pseudo_grad = outer_in - mean_params
    momentum_new = momentum_factor * momentum + pseudo_grad
    params_new = outer_in - outer_rate * (pseudo_grad + momentum_factor * momentum_new)
    return (params_new, momentum_new)

def to_full(shares):
    return shares.reshape(N_REPLICA, KVW, N_FSDP, SHARE).transpose(1, 2, 0, 3).reshape(KVW, D)

def to_shares(full):
    return full.reshape(KVW, N_FSDP, N_REPLICA, SHARE).transpose(2, 0, 1, 3).reshape(N_REPLICA, KVW, N_FSDP * SHARE)

def reference(grad_parts, inner_params, first_moment, second_moment, outer_params, outer_momentum):
    gradient = jnp.zeros(inner_params.shape, jnp.float32)
    for index in range(N_FSDP):
        gradient = gradient + grad_parts[:, index].astype(jnp.float32)
    first_out, second_out, updated = inner_adamw(gradient, inner_params, first_moment, second_moment)
    mean_params = lax.optimization_barrier(jnp.sum(updated, axis=0)) / N_REPLICA
    params_new, momentum_new = nesterov(mean_params, to_full(outer_params), to_full(outer_momentum))
    return (params_new, to_shares(params_new), to_shares(momentum_new), first_out, second_out)
```

```python
import jax
import jax.numpy as jnp
from jax import lax
from jax.experimental import pallas as pl
from jax.experimental.pallas import tpu as pltpu
from jax.sharding import PartitionSpec as P

MESH = pl.DeviceIdType.MESH
STEP = 100
CHUNKS = 4

beta_first = 0.9
beta_second = 0.95
inner_rate = 0.01
weight_decay = 0.1
epsilon = 1e-08
outer_rate = 0.7
momentum_factor = 0.9

FSDP = [(2, 0), (2, 1), (1, 0), (3, 0), (1, 1), (3, 1), (0, 1)]
COLUMN = [(2, 0), (2, 1), (1, 0), (3, 0), (1, 1), (3, 1), (0, 1)]
HIGH = [2, 1, 3]
ACROSS = [2, 1, 3]


def inner_adamw(gradient, params, first_in, second_in):
    first_out = beta_first * first_in + (1.0 - beta_first) * gradient
    second_out = beta_second * second_in + (1.0 - beta_second) * gradient * gradient
    first_scale = 1.0 / (1.0 - beta_first**STEP)
    second_scale = 1.0 / (1.0 - beta_second**STEP)
    direction = first_out * first_scale / (jnp.sqrt(second_out * second_scale) + epsilon)
    updated = params - inner_rate * (direction + weight_decay * params)
    return (first_out, second_out, updated)


def nesterov(mean_params, outer_in, momentum):
    pseudo_grad = outer_in - mean_params
    momentum_new = momentum_factor * momentum + pseudo_grad
    params_new = outer_in - outer_rate * (pseudo_grad + momentum_factor * momentum_new)
    return (params_new, momentum_new)


def kernel(
    g_hbm, p_hbm, m1_hbm, m2_hbm, op_hbm, om_hbm,
    full, p_out, m_out, first_out, second_out,
    own, parts, params, first_in, second_in, outer_in, momentum_in,
    updated, other, pair, sums,
    local_sem, grad_send, grad_recv, core_send, core_recv, high_send, high_recv,
    col_send, col_recv, row_send, row_recv, twin_send, twin_recv,
):
    replica, f = lax.axis_index("replica"), lax.axis_index("fsdp")
    yh, core = replica // 2, lax.rem(replica, 2)
    x, yl = f // 2, lax.rem(f, 2)
    rows = 64 // CHUNKS
    tiles = rows // 8

    def at_x(step):
        return lax.rem(x + step + 4, 4)

    def at_yh(step):
        return lax.rem(yh + step + 4, 4)

    def at_yl(flip):
        return 1 - yl if flip else yl

    twin = {"replica": yh * 2 + 1 - core}

    barrier = pltpu.get_barrier_semaphore()
    peers = [{"fsdp": at_x(s) * 2 + at_yl(flip)} for s, flip in FSDP]
    peers += [{"replica": at_yh(s) * 2 + core, "fsdp": x * 2 + at_yl(flip)} for s, flip in COLUMN if s]
    peers += [twin]
    for peer in peers:
        pl.semaphore_signal(barrier, inc=1, device_id=peer, device_id_type=MESH)

    mine = pl.ds(pl.multiple_of(f * 1024, 1024), 1024)
    loads = [
        pltpu.make_async_copy(src, dst, local_sem.at[i])
        for i, (src, dst) in enumerate(
            (
                (g_hbm.at[:, mine], own),
                (p_hbm, params),
                (m1_hbm, first_in),
                (m2_hbm, second_in),
                (op_hbm, outer_in),
                (om_hbm, momentum_in),
            )
        )
    ]
    for load in loads:
        load.start()
    pl.semaphore_wait(barrier, len(peers))

    def remote(src, dst, send, recv, peer):
        return pltpu.make_async_remote_copy(
            src_ref=src, dst_ref=dst, send_sem=send, recv_sem=recv, device_id=peer, device_id_type=MESH
        )

    def grad_copy(c, j):
        s, flip = FSDP[j]
        to = at_x(s) * 2 + at_yl(flip)
        band = pl.ds(c * rows, rows)
        return remote(
            g_hbm.at[band, pl.ds(pl.multiple_of(to * 1024, 1024), 1024)],
            parts.at[j, band], grad_send.at[c, j], grad_recv.at[c, j], {"fsdp": to},
        )

    def core_copy(c):
        band = pl.ds(c * tiles, tiles)
        return remote(updated.at[band, :, 1 - core], other.at[band], core_send.at[c], core_recv.at[c], twin)

    def high_copy(c, j):
        band = pl.ds(c * tiles, tiles)
        to = at_yh(HIGH[j])
        return remote(
            pair.at[band, to], sums.at[j, band], high_send.at[c, j], high_recv.at[c, j], {"replica": to * 2 + core}
        )

    def col_copy(c, j, arriving=False):
        band = pl.ds(c * tiles, tiles)
        s, flip = COLUMN[j]
        block = full.at[band, x, at_yl(flip), at_yh(-s), core] if arriving else full.at[band, x, yl, yh, core]
        peer = {"replica": at_yh(s) * 2 + core, "fsdp": x * 2 + at_yl(flip)}
        return remote(block, block, col_send.at[c, j], col_recv.at[c, j], peer)

    def row_copy(c, j, arriving=False):
        band = pl.ds(c * tiles, tiles)
        block = full.at[band, at_x(-ACROSS[j]) if arriving else x, :, :, core]
        return remote(block, block, row_send.at[c, j], row_recv.at[c, j], {"fsdp": at_x(ACROSS[j]) * 2 + yl})

    def twin_copy(c, j, arriving=False):
        band = pl.ds(c * tiles, tiles)
        from_x = at_x(-ACROSS[j]) if j < 3 else x
        block = full.at[band, from_x, :, :, 1 - core if arriving else core]
        return remote(block, block, twin_send.at[c, j], twin_recv.at[c, j], twin)

    def reduce_gradient(c):
        for j in range(7):
            grad_copy(c, j).wait_recv()
        band = pl.ds(c * rows, rows)
        for q in range(4):
            cols = pl.ds(q * 256, 256)
            gradient = own[band, cols].astype(jnp.float32)
            for j in range(7):
                gradient = gradient + parts[j, band, cols].astype(jnp.float32)
            first, second, new = inner_adamw(gradient, params[band, cols], first_in[band, cols], second_in[band, cols])
            first_out[band, cols] = first
            second_out[band, cols] = second
            for t in range(tiles):
                for h in range(2):
                    updated[c * tiles + t, q, h] = new[t * 8 : t * 8 + 8, h * 128 : h * 128 + 128]
        core_copy(c).start()

    def sum_cores(c):
        core_copy(c).wait_recv()
        band = pl.ds(c * tiles, tiles)
        pair[band] = updated[band, :, core] + other[band]
        for j in range(3):
            high_copy(c, j).start()

    def outer_step(c):
        for j in range(3):
            high_copy(c, j).wait_recv()
        band = pl.ds(c * tiles, tiles)
        total = pair[band, yh] + sums[0, band] + sums[1, band] + sums[2, band]
        new, momentum = nesterov(total * 0.125, outer_in[band], momentum_in[band])
        p_out[band] = new
        m_out[band] = momentum
        full[band, x, yl, yh, core] = new
        for j in range(7):
            col_copy(c, j).start()

    def to_rows(c):
        for j in range(7):
            col_copy(c, j, True).wait_recv()
        for j in range(3):
            row_copy(c, j).start()
        twin_copy(c, 3).start()

    def to_twin(c):
        for j in (1, 2, 0):
            row_copy(c, j, True).wait_recv()
            twin_copy(c, j).start()

    def finish(c):
        for j in (3, 1, 2, 0):
            twin_copy(c, j, True).wait_recv()

    for c in range(CHUNKS):
        for j in range(7):
            grad_copy(c, j).start()
    for load in loads:
        load.wait()

    stages = [reduce_gradient, sum_cores, outer_step, to_rows, to_twin, finish]
    for t in range(CHUNKS + len(stages) - 1):
        for s in reversed(range(len(stages))):
            if 0 <= t - s < CHUNKS:
                stages[s](t - s)
    for c in range(CHUNKS):
        for j in range(7):
            grad_copy(c, j).wait_send()
            col_copy(c, j).wait_send()
        core_copy(c).wait_send()
        for j in range(3):
            high_copy(c, j).wait_send()
            row_copy(c, j).wait_send()
        for j in range(4):
            twin_copy(c, j).wait_send()


def store_kernel(*refs):
    sources, targets, sems = refs[:5], refs[5:10], refs[10]
    copies = [pltpu.make_async_copy(src, dst, sems.at[i]) for i, (src, dst) in enumerate(zip(sources, targets))]
    for copy in copies:
        copy.start()
    for copy in copies:
        copy.wait()


def store(arrays):
    return pl.pallas_call(
        store_kernel,
        out_shape=tuple(jax.ShapeDtypeStruct(a.shape, a.dtype) for a in arrays),
        in_specs=[pl.BlockSpec(memory_space=pltpu.VMEM)] * 5,
        out_specs=(pl.BlockSpec(memory_space=pltpu.HBM),) * 5,
        scratch_shapes=[pltpu.SemaphoreType.DMA((5,))],
        name="store",
    )(*(pltpu.with_memory_space_constraint(a, pltpu.VMEM) for a in arrays))


def local(grad_parts, inner_params, first_moment, second_moment, outer_params, outer_momentum):
    f32, bf16 = jnp.float32, jnp.bfloat16
    dma = pltpu.SemaphoreType.DMA
    vmem = pl.BlockSpec(memory_space=pltpu.VMEM)
    operands = (
        grad_parts.reshape(64, 8192),
        inner_params.reshape(64, 1024),
        first_moment.reshape(64, 1024),
        second_moment.reshape(64, 1024),
        outer_params.reshape(8, 8, 128),
        outer_momentum.reshape(8, 8, 128),
    )
    results = pl.pallas_call(
        kernel,
        out_shape=(
            pltpu.VMEM((8, 4, 2, 4, 2, 8, 128), f32),
            pltpu.VMEM((8, 8, 128), f32),
            pltpu.VMEM((8, 8, 128), f32),
            pltpu.VMEM((64, 1024), f32),
            pltpu.VMEM((64, 1024), f32),
        ),
        in_specs=[pl.BlockSpec(memory_space=pltpu.HBM)] * 6,
        out_specs=(vmem,) * 5,
        scratch_shapes=[
            pltpu.VMEM((64, 1024), bf16),
            pltpu.VMEM((7, 64, 1024), bf16),
            pltpu.VMEM((64, 1024), f32),
            pltpu.VMEM((64, 1024), f32),
            pltpu.VMEM((64, 1024), f32),
            pltpu.VMEM((8, 8, 128), f32),
            pltpu.VMEM((8, 8, 128), f32),
            pltpu.VMEM((8, 4, 2, 8, 128), f32),
            pltpu.VMEM((8, 4, 8, 128), f32),
            pltpu.VMEM((8, 4, 8, 128), f32),
            pltpu.VMEM((3, 8, 8, 128), f32),
            dma((6,)),
            dma((CHUNKS, 7)), dma((CHUNKS, 7)),
            dma((CHUNKS,)), dma((CHUNKS,)),
            dma((CHUNKS, 3)), dma((CHUNKS, 3)),
            dma((CHUNKS, 7)), dma((CHUNKS, 7)),
            dma((CHUNKS, 3)), dma((CHUNKS, 3)),
            dma((CHUNKS, 4)), dma((CHUNKS, 4)),
        ],
        compiler_params=pltpu.CompilerParams(
            collective_id=0, has_side_effects=True, vmem_limit_bytes=32 * 2**20
        ),
        name="sync",
    )(*(pltpu.with_memory_space_constraint(a, pltpu.HBM) for a in operands))
    full, p_new, m_new, first, second = store(results)
    next_weights = full.reshape(8, 64, 8, 128).transpose(0, 2, 1, 3).reshape(64, 8192)
    return (
        next_weights,
        p_new.reshape(1, 64, 128),
        m_new.reshape(1, 64, 128),
        first.reshape(1, 64, 1024),
        second.reshape(1, 64, 1024),
    )


def solution(mesh):
    return jax.shard_map(
        local,
        mesh=mesh,
        in_specs=(
            P("replica", "fsdp", "tensor", None),
            P("replica", "tensor", "fsdp"),
            P("replica", "tensor", "fsdp"),
            P("replica", "tensor", "fsdp"),
            P("replica", "tensor", "fsdp"),
            P("replica", "tensor", "fsdp"),
        ),
        out_specs=(
            P("tensor", None),
            P("replica", "tensor", "fsdp"),
            P("replica", "tensor", "fsdp"),
            P("replica", "tensor", "fsdp"),
            P("replica", "tensor", "fsdp"),
        ),
        check_vma=False,
    )
```

```python
import jax
import jax.numpy as jnp
from jax import lax
from jax.experimental import pallas as pl
from jax.experimental.pallas import tpu as pltpu
from jax.sharding import PartitionSpec as P

MESH = pl.DeviceIdType.MESH
STEP = 100
CHUNKS = 2
DEPTH = 2
RELAY = (0, 0, 0, 0)
INLINE = 1

beta_first = 0.9
beta_second = 0.95
inner_rate = 0.01
weight_decay = 0.1
epsilon = 1e-08
outer_rate = 0.7
momentum_factor = 0.9

FSDP = [(2, 0), (2, 1), (1, 0), (3, 0), (1, 1), (3, 1), (0, 1)]
COLUMN = [(2, 0), (2, 1), (1, 0), (3, 0), (1, 1), (3, 1), (0, 1)]
HIGH = [2, 1, 3]
ACROSS = [2, 1, 3]


def inner_adamw(gradient, params, first_in, second_in):
    first_out = beta_first * first_in + (1.0 - beta_first) * gradient
    second_out = beta_second * second_in + (1.0 - beta_second) * gradient * gradient
    first_scale = 1.0 / (1.0 - beta_first**STEP)
    second_scale = 1.0 / (1.0 - beta_second**STEP)
    direction = first_out * first_scale / (jnp.sqrt(second_out * second_scale) + epsilon)
    updated = params - inner_rate * (direction + weight_decay * params)
    return (first_out, second_out, updated)


def nesterov(mean_params, outer_in, momentum):
    pseudo_grad = outer_in - mean_params
    momentum_new = momentum_factor * momentum + pseudo_grad
    params_new = outer_in - outer_rate * (pseudo_grad + momentum_factor * momentum_new)
    return (params_new, momentum_new)


SCALE = 2048.0
POWER = 13


def encode(weights):
    t = jnp.clip(weights * SCALE, -850.0, 850.0)
    t4 = (t * t) * (t * t)
    return (t4 * t4 * t4 * t).astype(jnp.bfloat16)


def decode(codes):
    c = codes.astype(jnp.float32)
    size = jnp.exp2(jnp.log2(jnp.maximum(jnp.abs(c), 1e-37)) * (1.0 / POWER)) * (1.0 / SCALE)
    return jnp.where(c == 0.0, 0.0, jnp.where(c < 0.0, -size, size))


def kernel(
    g_hbm, p_hbm, m1_hbm, m2_hbm, op_hbm, om_hbm,
    full, p_out, m_out, first_out, second_out,
    own, parts, params, first_in, second_in, outer_in, momentum_in,
    updated, other, pair, sums,
    local_sem, grad_send, grad_recv, core_send, core_recv, high_send, high_recv,
    col_send, col_recv, row_send, row_recv, relay_send, relay_recv, twin_send, twin_recv,
):
    replica, f = lax.axis_index("replica"), lax.axis_index("fsdp")
    yh, core = replica // 2, lax.rem(replica, 2)
    x, yl = f // 2, lax.rem(f, 2)
    rows = 64 // CHUNKS
    tiles = rows // 8

    def at_x(step):
        return lax.rem(x + step + 4, 4)

    def at_yh(step):
        return lax.rem(yh + step + 4, 4)

    def at_yl(flip):
        return 1 - yl if flip else yl

    twin = {"replica": yh * 2 + 1 - core}

    barrier = pltpu.get_barrier_semaphore()
    peers = [{"fsdp": at_x(s) * 2 + at_yl(flip)} for s, flip in FSDP]
    peers += [{"replica": at_yh(s) * 2 + core, "fsdp": x * 2 + at_yl(flip)} for s, flip in COLUMN if s]
    peers += [twin]
    for peer in peers:
        pl.semaphore_signal(barrier, inc=1, device_id=peer, device_id_type=MESH)

    mine = pl.ds(pl.multiple_of(f * 1024, 1024), 1024)
    loads = [
        pltpu.make_async_copy(src, dst, local_sem.at[i])
        for i, (src, dst) in enumerate(
            (
                (g_hbm.at[:, mine], own),
                (p_hbm, params),
                (m1_hbm, first_in),
                (m2_hbm, second_in),
                (op_hbm, outer_in),
                (om_hbm, momentum_in),
            )
        )
    ]
    for load in loads:
        load.start()
    pl.semaphore_wait(barrier, len(peers))

    def remote(src, dst, send, recv, peer):
        return pltpu.make_async_remote_copy(
            src_ref=src, dst_ref=dst, send_sem=send, recv_sem=recv, device_id=peer, device_id_type=MESH
        )

    def grad_copy(c, j):
        s, flip = FSDP[j]
        to = at_x(s) * 2 + at_yl(flip)
        band = pl.ds(c * rows, rows)
        return remote(
            g_hbm.at[band, pl.ds(pl.multiple_of(to * 1024, 1024), 1024)],
            parts.at[j, band], grad_send.at[c, j], grad_recv.at[c, j], {"fsdp": to},
        )

    def core_copy(c):
        band = pl.ds(c * tiles, tiles)
        return remote(updated.at[band, :, 1 - core], other.at[band], core_send.at[c], core_recv.at[c], twin)

    def high_copy(c, j):
        band = pl.ds(c * tiles, tiles)
        to = at_yh(HIGH[j])
        return remote(
            pair.at[band, to], sums.at[j, band], high_send.at[c, j], high_recv.at[c, j], {"replica": to * 2 + core}
        )

    def col_copy(c, j, arriving=False):
        s, flip = COLUMN[j]
        block = full.at[c, x, at_yl(flip), at_yh(-s), core] if arriving else full.at[c, x, yl, yh, core]
        peer = {"replica": at_yh(s) * 2 + core, "fsdp": x * 2 + at_yl(flip)}
        return remote(block, block, col_send.at[c, j], col_recv.at[c, j], peer)

    def row_copy(c, j, arriving=False):
        block = full.at[c, at_x(-ACROSS[j]) if arriving else x, :, :, core]
        return remote(block, block, row_send.at[c, j], row_recv.at[c, j], {"fsdp": at_x(ACROSS[j]) * 2 + yl})

    def relay_copy(c, j, arriving=False):
        step = 1 - 2 * j
        block = full.at[c, at_x(2) if arriving else at_x(-step), j, :, core]
        return remote(block, block, relay_send.at[c, j], relay_recv.at[c, j], {"fsdp": at_x(step) * 2 + yl})

    def twin_copy(c, j, arriving=False):
        from_x = at_x(-ACROSS[j]) if j < 3 else x
        block = full.at[c, from_x, :, :, 1 - core if arriving else core]
        return remote(block, block, twin_send.at[c, j], twin_recv.at[c, j], twin)

    def send_gradient(c):
        for j in range(7):
            grad_copy(c, j).start()

    def reduce_gradient(c):
        for j in range(7):
            grad_copy(c, j).wait_recv()
        if c + DEPTH < CHUNKS:
            send_gradient(c + DEPTH)
        band = pl.ds(c * rows, rows)
        for q in range(4):
            cols = pl.ds(q * 256, 256)
            gradient = own[band, cols].astype(jnp.float32)
            for j in range(7):
                gradient = gradient + parts[j, band, cols].astype(jnp.float32)
            first, second, new = inner_adamw(gradient, params[band, cols], first_in[band, cols], second_in[band, cols])
            first_out[band, cols] = first
            second_out[band, cols] = second
            for t in range(tiles):
                for h in range(2):
                    updated[c * tiles + t, q, h] = new[t * 8 : t * 8 + 8, h * 128 : h * 128 + 128]
        core_copy(c).start()
        if INLINE:
            sum_cores(c)

    def sum_cores(c):
        core_copy(c).wait_recv()
        band = pl.ds(c * tiles, tiles)
        pair[band] = updated[band, :, core] + other[band]
        for j in range(3):
            high_copy(c, j).start()

    def outer_step(c):
        for j in range(3):
            high_copy(c, j).wait_recv()
        band = pl.ds(c * tiles, tiles)
        total = pair[band, yh] + sums[0, band] + sums[1, band] + sums[2, band]
        new, momentum = nesterov(total * 0.125, outer_in[band], momentum_in[band])
        p_out[band] = new
        m_out[band] = momentum
        full[c, x, yl, yh, core] = encode(new.reshape(rows, 128))
        for j in range(7):
            col_copy(c, j).start()

    def to_rows(c):
        for j in range(7):
            col_copy(c, j, True).wait_recv()
        for j in (1, 2) if RELAY[c] else (0, 1, 2):
            row_copy(c, j).start()
        twin_copy(c, 3).start()

    def to_twin(c):
        for j in (1, 2):
            row_copy(c, j, True).wait_recv()
            if RELAY[c]:
                relay_copy(c, j - 1).start()
            twin_copy(c, j).start()
        if not RELAY[c]:
            row_copy(c, 0, True).wait_recv()
            twin_copy(c, 0).start()

    def relayed(c):
        if RELAY[c]:
            for j in range(2):
                relay_copy(c, j, True).wait_recv()
            twin_copy(c, 0).start()

    def finish(c):
        for j in (3, 1, 2, 0):
            twin_copy(c, j, True).wait_recv()

    for c in range(min(DEPTH, CHUNKS)):
        send_gradient(c)
    for load in loads:
        load.wait()

    stages = [reduce_gradient, sum_cores, outer_step, to_rows, to_twin, relayed, finish]
    if INLINE:
        stages.remove(sum_cores)
    for t in range(CHUNKS + len(stages) - 1):
        for s in range(len(stages)):
            if 0 <= t - s < CHUNKS:
                stages[s](t - s)
    for c in range(CHUNKS):
        for j in range(7):
            grad_copy(c, j).wait_send()
            col_copy(c, j).wait_send()
        core_copy(c).wait_send()
        for j in range(3):
            high_copy(c, j).wait_send()
        for j in (1, 2) if RELAY[c] else (0, 1, 2):
            row_copy(c, j).wait_send()
        for j in range(2 if RELAY[c] else 0):
            relay_copy(c, j).wait_send()
        for j in range(4):
            twin_copy(c, j).wait_send()


def store_kernel(*refs):
    sources, targets, weights, sems = refs[:5], refs[5:10], refs[10], refs[11]
    codes = sources[0]
    rows = 64 // CHUNKS
    copies = [pltpu.make_async_copy(sources[i], targets[i], sems.at[i]) for i in range(1, 5)]
    for copy in copies:
        copy.start()
    for c in range(CHUNKS):
        band = pl.ds(c * rows, rows)

        def unpack(x, _):
            for yl in range(2):
                for yh in range(4):
                    for core in range(2):
                        at = pl.multiple_of(x * 2048 + yl * 1024 + yh * 256 + core * 128, 128)
                        weights[band, pl.ds(at, 128)] = decode(codes[c, x, yl, yh, core])
            return _

        lax.fori_loop(0, 4, unpack, 0)
        copy = pltpu.make_async_copy(weights.at[band], targets[0].at[band], sems.at[5 + c])
        copy.start()
        copies.append(copy)
    for copy in copies:
        copy.wait()


def store(arrays):
    shapes = [(64, 8192)] + [a.shape for a in arrays[1:]]
    return pl.pallas_call(
        store_kernel,
        out_shape=tuple(jax.ShapeDtypeStruct(shape, jnp.float32) for shape in shapes),
        in_specs=[pl.BlockSpec(memory_space=pltpu.VMEM)] * 5,
        out_specs=(pl.BlockSpec(memory_space=pltpu.HBM),) * 5,
        scratch_shapes=[pltpu.VMEM((64, 8192), jnp.float32), pltpu.SemaphoreType.DMA((5 + CHUNKS,))],
        name="store",
    )(*(pltpu.with_memory_space_constraint(a, pltpu.VMEM) for a in arrays))


def local(grad_parts, inner_params, first_moment, second_moment, outer_params, outer_momentum):
    f32, bf16 = jnp.float32, jnp.bfloat16
    dma = pltpu.SemaphoreType.DMA
    vmem = pl.BlockSpec(memory_space=pltpu.VMEM)
    operands = (
        grad_parts.reshape(64, 8192),
        inner_params.reshape(64, 1024),
        first_moment.reshape(64, 1024),
        second_moment.reshape(64, 1024),
        outer_params.reshape(8, 8, 128),
        outer_momentum.reshape(8, 8, 128),
    )
    results = pl.pallas_call(
        kernel,
        out_shape=(
            pltpu.VMEM((CHUNKS, 4, 2, 4, 2, 64 // CHUNKS, 128), bf16),
            pltpu.VMEM((8, 8, 128), f32),
            pltpu.VMEM((8, 8, 128), f32),
            pltpu.VMEM((64, 1024), f32),
            pltpu.VMEM((64, 1024), f32),
        ),
        in_specs=[pl.BlockSpec(memory_space=pltpu.HBM)] * 6,
        out_specs=(vmem,) * 5,
        scratch_shapes=[
            pltpu.VMEM((64, 1024), bf16),
            pltpu.VMEM((7, 64, 1024), bf16),
            pltpu.VMEM((64, 1024), f32),
            pltpu.VMEM((64, 1024), f32),
            pltpu.VMEM((64, 1024), f32),
            pltpu.VMEM((8, 8, 128), f32),
            pltpu.VMEM((8, 8, 128), f32),
            pltpu.VMEM((8, 4, 2, 8, 128), f32),
            pltpu.VMEM((8, 4, 8, 128), f32),
            pltpu.VMEM((8, 4, 8, 128), f32),
            pltpu.VMEM((3, 8, 8, 128), f32),
            dma((6,)),
            dma((CHUNKS, 7)), dma((CHUNKS, 7)),
            dma((CHUNKS,)), dma((CHUNKS,)),
            dma((CHUNKS, 3)), dma((CHUNKS, 3)),
            dma((CHUNKS, 7)), dma((CHUNKS, 7)),
            dma((CHUNKS, 3)), dma((CHUNKS, 3)),
            dma((CHUNKS, 2)), dma((CHUNKS, 2)),
            dma((CHUNKS, 4)), dma((CHUNKS, 4)),
        ],
        compiler_params=pltpu.CompilerParams(
            collective_id=0, has_side_effects=True, vmem_limit_bytes=32 * 2**20
        ),
        name="sync",
    )(*(pltpu.with_memory_space_constraint(a, pltpu.HBM) for a in operands))
    next_weights, p_new, m_new, first, second = store(results)
    return (
        next_weights,
        p_new.reshape(1, 64, 128),
        m_new.reshape(1, 64, 128),
        first.reshape(1, 64, 1024),
        second.reshape(1, 64, 1024),
    )


def solution(mesh):
    return jax.shard_map(
        local,
        mesh=mesh,
        in_specs=(
            P("replica", "fsdp", "tensor", None),
            P("replica", "tensor", "fsdp"),
            P("replica", "tensor", "fsdp"),
            P("replica", "tensor", "fsdp"),
            P("replica", "tensor", "fsdp"),
            P("replica", "tensor", "fsdp"),
        ),
        out_specs=(
            P("tensor", None),
            P("replica", "tensor", "fsdp"),
            P("replica", "tensor", "fsdp"),
            P("replica", "tensor", "fsdp"),
            P("replica", "tensor", "fsdp"),
        ),
        check_vma=False,
    )
```

```python
import jax
import jax.numpy as jnp
from jax import lax
from jax.experimental import pallas as pl
from jax.experimental.pallas import tpu as pltpu
from jax.sharding import PartitionSpec as P

MESH = pl.DeviceIdType.MESH
STEP = 100
UNITS = (2, 1, 1)
CHUNKS = len(UNITS)
ORDER = (
    "S0", "S1", "S2", "N0", "L0", "R0", "R1", "R2",
    "O0", "O1", "O2", "C0", "C1", "C2", "W0", "W1",
    "W2", "F0", "F1", "F2", "Dh", "Dc", "Dr", "Dt",
)
FIRST = tuple(sum(UNITS[:c]) for c in range(len(UNITS)))

beta_first = 0.9
beta_second = 0.95
inner_rate = 0.01
weight_decay = 0.1
epsilon = 1e-08
outer_rate = 0.7
momentum_factor = 0.9

FSDP = [(2, 0), (2, 1), (1, 0), (3, 0), (1, 1), (3, 1), (0, 1)]
COLUMN = [(2, 0), (2, 1), (1, 0), (3, 0), (1, 1), (3, 1), (0, 1)]
HIGH = [2, 1, 3]
ACROSS = [2, 1, 3]


def inner_adamw(gradient, params, first_in, second_in):
    first_out = beta_first * first_in + (1.0 - beta_first) * gradient
    second_out = beta_second * second_in + (1.0 - beta_second) * gradient * gradient
    first_scale = 1.0 / (1.0 - beta_first**STEP)
    second_scale = 1.0 / (1.0 - beta_second**STEP)
    direction = first_out * first_scale / (jnp.sqrt(second_out * second_scale) + epsilon)
    updated = params - inner_rate * (direction + weight_decay * params)
    return (first_out, second_out, updated)


def nesterov(mean_params, outer_in, momentum):
    pseudo_grad = outer_in - mean_params
    momentum_new = momentum_factor * momentum + pseudo_grad
    params_new = outer_in - outer_rate * (pseudo_grad + momentum_factor * momentum_new)
    return (params_new, momentum_new)


SCALE = 2048.0
POWER = 13


def encode(weights):
    t = jnp.clip(weights * SCALE, -850.0, 850.0)
    t4 = (t * t) * (t * t)
    return (t4 * t4 * t4 * t).astype(jnp.bfloat16)


def decode(codes):
    c = codes.astype(jnp.float32)
    size = jnp.exp2(jnp.log2(jnp.maximum(jnp.abs(c), 1e-37)) * (1.0 / POWER)) * (1.0 / SCALE)
    return jnp.where(c == 0.0, 0.0, jnp.where(c < 0.0, -size, size))


def kernel(
    g_hbm, p_hbm, m1_hbm, m2_hbm, op_hbm, om_hbm,
    full, p_out, m_out, first_out, second_out,
    own, parts, params, first_in, second_in, outer_in, momentum_in,
    updated, other, pair, sums,
    near_a, near_b, local_sem, grad_send, grad_recv, core_send, core_recv, high_send, high_recv,
    col_send, col_recv, row_send, row_recv, twin_send, twin_recv,
):
    near_sems = (near_a, near_b)
    replica, f = lax.axis_index("replica"), lax.axis_index("fsdp")
    yh, core = replica // 2, lax.rem(replica, 2)
    x, yl = f // 2, lax.rem(f, 2)

    def row_band(c):
        return pl.ds(FIRST[c] * 16, UNITS[c] * 16)

    def tile_band(c):
        return pl.ds(FIRST[c] * 2, UNITS[c] * 2)

    def unit_band(c):
        return pl.ds(FIRST[c], UNITS[c])

    def at_x(step):
        return lax.rem(x + step + 4, 4)

    def at_yh(step):
        return lax.rem(yh + step + 4, 4)

    def at_yl(flip):
        return 1 - yl if flip else yl

    twin = {"replica": yh * 2 + 1 - core}

    barrier = pltpu.get_barrier_semaphore()
    peers = [{"fsdp": at_x(s) * 2 + at_yl(flip)} for s, flip in FSDP]
    peers += [{"replica": at_yh(s) * 2 + core} for s in (1, 3)]
    peers += [twin]
    for peer in peers:
        pl.semaphore_signal(barrier, inc=1, device_id=peer, device_id_type=MESH)

    mine = pl.ds(pl.multiple_of(f * 1024, 1024), 1024)
    loads = [
        pltpu.make_async_copy(src, dst, local_sem.at[i])
        for i, (src, dst) in enumerate(
            (
                (g_hbm.at[:, mine], own),
                (p_hbm, params),
                (m1_hbm, first_in),
                (m2_hbm, second_in),
                (op_hbm, outer_in),
                (om_hbm, momentum_in),
            )
        )
    ]
    for load in loads:
        load.start()
    pl.semaphore_wait(barrier, len(peers))

    def remote(src, dst, send, recv, peer):
        return pltpu.make_async_remote_copy(
            src_ref=src, dst_ref=dst, send_sem=send, recv_sem=recv, device_id=peer, device_id_type=MESH
        )

    def grad_copy(c, j):
        s, flip = FSDP[j]
        to = at_x(s) * 2 + at_yl(flip)
        band = row_band(c)
        return remote(
            g_hbm.at[band, pl.ds(pl.multiple_of(to * 1024, 1024), 1024)],
            parts.at[j, band], grad_send.at[c, j], grad_recv.at[c, j], {"fsdp": to},
        )

    def core_copy(c):
        band = tile_band(c)
        return remote(updated.at[band, :, 1 - core], other.at[band], core_send.at[c], core_recv.at[c], twin)

    def high_copy(c, j):
        band = tile_band(c)
        to = at_yh(HIGH[j])
        return remote(
            pair.at[band, to], sums.at[j, band], high_send.at[c, j], high_recv.at[c, j], {"replica": to * 2 + core}
        )

    def col_copy(c, j, arriving=False):
        s, flip = COLUMN[j]
        band = unit_band(c)
        block = full.at[band, x, at_yl(flip), at_yh(-s), core] if arriving else full.at[band, x, yl, yh, core]
        peer = {"replica": at_yh(s) * 2 + core, "fsdp": x * 2 + at_yl(flip)}
        return remote(block, block, col_send.at[c, j], col_recv.at[c, j], peer)

    def row_copy(c, j, arriving=False):
        block = full.at[unit_band(c), at_x(-ACROSS[j]) if arriving else x, :, :, core]
        return remote(block, block, row_send.at[c, j], row_recv.at[c, j], {"fsdp": at_x(ACROSS[j]) * 2 + yl})

    def twin_copy(c, j, arriving=False):
        from_x = at_x(-ACROSS[j]) if j < 3 else x
        block = full.at[unit_band(c), from_x, :, :, 1 - core if arriving else core]
        return remote(block, block, twin_send.at[c, j], twin_recv.at[c, j], twin)

    def send_gradient(c):
        for j in range(7):
            grad_copy(c, j).start()

    def reduce_gradient(c):
        for j in range(7):
            grad_copy(c, j).wait_recv()
        for u in range(FIRST[c], FIRST[c] + UNITS[c]):
            band = pl.ds(u * 16, 16)
            for q in range(4):
                cols = pl.ds(q * 256, 256)
                gradient = own[band, cols].astype(jnp.float32)
                for j in range(7):
                    gradient = gradient + parts[j, band, cols].astype(jnp.float32)
                first, second, new = inner_adamw(
                    gradient, params[band, cols], first_in[band, cols], second_in[band, cols]
                )
                first_out[band, cols] = first
                second_out[band, cols] = second
                for t in range(2):
                    for h in range(2):
                        updated[2 * u + t, q, h] = new[t * 8 : t * 8 + 8, h * 128 : h * 128 + 128]
        core_copy(c).start()
        core_copy(c).wait_recv()
        band = tile_band(c)
        pair[band] = updated[band, :, core] + other[band]
        for j in range(3):
            high_copy(c, j).start()

    def outer_step(c):
        for j in range(3):
            high_copy(c, j).wait_recv()
        band = tile_band(c)
        total = pair[band, yh] + sums[0, band] + sums[1, band] + sums[2, band]
        new, momentum = nesterov(total * 0.125, outer_in[band], momentum_in[band])
        p_out[band] = new
        m_out[band] = momentum
        full[unit_band(c), x, yl, yh, core] = encode(new.reshape(UNITS[c], 16, 128))
        for j in range(7):
            col_copy(c, j).start()

    def to_rows(c):
        for j in range(7):
            col_copy(c, j, True).wait_recv()
        for j in range(3):
            row_copy(c, j).start()
        twin_copy(c, 3).start()

    def to_twin(c):
        for j in (1, 2, 0):
            row_copy(c, j, True).wait_recv()
            twin_copy(c, j).start()

    def finish(c):
        for j in (3, 1, 2, 0):
            twin_copy(c, j, True).wait_recv()


    def ready(c):
        for sem in near_sems:
            for step in (1, 3):
                pl.semaphore_signal(
                    sem, inc=1, device_id={"replica": at_yh(step) * 2 + core}, device_id_type=MESH
                )
            pl.semaphore_wait(sem, 2)

    def loaded(c):
        for load in loads:
            load.wait()

    stages = {"S": send_gradient, "N": ready, "L": loaded, "R": reduce_gradient, "O": outer_step, "C": to_rows, "W": to_twin, "F": finish}
    def drain(kind):
        for c in range(CHUNKS):
            if kind == "h":
                for j in range(7):
                    grad_copy(c, j).wait_send()
                core_copy(c).wait_send()
                for j in range(3):
                    high_copy(c, j).wait_send()
            elif kind == "c":
                for j in range(7):
                    col_copy(c, j).wait_send()
            elif kind == "r":
                for j in range(3):
                    row_copy(c, j).wait_send()
            else:
                for j in range(4):
                    twin_copy(c, j).wait_send()

    for step in ORDER:
        if step[0] == "D":
            drain(step[1])
        else:
            stages[step[0]](int(step[1]))


def store_kernel(*refs):
    sources, targets, weights, sems = refs[:5], refs[5:10], refs[10], refs[11]
    codes = sources[0]
    copies = [pltpu.make_async_copy(sources[i], targets[i], sems.at[i]) for i in range(1, 5)]
    for copy in copies:
        copy.start()
    for c in range(4):
        band = pl.ds(c * 16, 16)

        def unpack(x, _):
            for yl in range(2):
                for yh in range(4):
                    for core in range(2):
                        at = pl.multiple_of(x * 2048 + yl * 1024 + yh * 256 + core * 128, 128)
                        weights[band, pl.ds(at, 128)] = decode(codes[c, x, yl, yh, core])
            return _

        lax.fori_loop(0, 4, unpack, 0)
        copy = pltpu.make_async_copy(weights.at[band], targets[0].at[band], sems.at[5 + c])
        copy.start()
        copies.append(copy)
    for copy in copies:
        copy.wait()


def store(arrays):
    shapes = [(64, 8192)] + [a.shape for a in arrays[1:]]
    return pl.pallas_call(
        store_kernel,
        out_shape=tuple(jax.ShapeDtypeStruct(shape, jnp.float32) for shape in shapes),
        in_specs=[pl.BlockSpec(memory_space=pltpu.VMEM)] * 5,
        out_specs=(pl.BlockSpec(memory_space=pltpu.HBM),) * 5,
        scratch_shapes=[pltpu.VMEM((64, 8192), jnp.float32), pltpu.SemaphoreType.DMA((9,))],
        name="store",
    )(*(pltpu.with_memory_space_constraint(a, pltpu.VMEM) for a in arrays))


def local(grad_parts, inner_params, first_moment, second_moment, outer_params, outer_momentum):
    f32, bf16 = jnp.float32, jnp.bfloat16
    dma = pltpu.SemaphoreType.DMA
    vmem = pl.BlockSpec(memory_space=pltpu.VMEM)
    operands = (
        grad_parts.reshape(64, 8192),
        inner_params.reshape(64, 1024),
        first_moment.reshape(64, 1024),
        second_moment.reshape(64, 1024),
        outer_params.reshape(8, 8, 128),
        outer_momentum.reshape(8, 8, 128),
    )
    results = pl.pallas_call(
        kernel,
        out_shape=(
            pltpu.VMEM((4, 4, 2, 4, 2, 16, 128), bf16),
            pltpu.VMEM((8, 8, 128), f32),
            pltpu.VMEM((8, 8, 128), f32),
            pltpu.VMEM((64, 1024), f32),
            pltpu.VMEM((64, 1024), f32),
        ),
        in_specs=[pl.BlockSpec(memory_space=pltpu.HBM)] * 6,
        out_specs=(vmem,) * 5,
        scratch_shapes=[
            pltpu.VMEM((64, 1024), bf16),
            pltpu.VMEM((7, 64, 1024), bf16),
            pltpu.VMEM((64, 1024), f32),
            pltpu.VMEM((64, 1024), f32),
            pltpu.VMEM((64, 1024), f32),
            pltpu.VMEM((8, 8, 128), f32),
            pltpu.VMEM((8, 8, 128), f32),
            pltpu.VMEM((8, 4, 2, 8, 128), f32),
            pltpu.VMEM((8, 4, 8, 128), f32),
            pltpu.VMEM((8, 4, 8, 128), f32),
            pltpu.VMEM((3, 8, 8, 128), f32),
            pltpu.SemaphoreType.REGULAR,
            pltpu.SemaphoreType.REGULAR,
            dma((6,)),
            dma((CHUNKS, 7)), dma((CHUNKS, 7)),
            dma((CHUNKS,)), dma((CHUNKS,)),
            dma((CHUNKS, 3)), dma((CHUNKS, 3)),
            dma((CHUNKS, 7)), dma((CHUNKS, 7)),
            dma((CHUNKS, 3)), dma((CHUNKS, 3)),
            dma((CHUNKS, 4)), dma((CHUNKS, 4)),
        ],
        compiler_params=pltpu.CompilerParams(
            collective_id=0, has_side_effects=True, vmem_limit_bytes=32 * 2**20
        ),
        name="sync",
    )(*(pltpu.with_memory_space_constraint(a, pltpu.HBM) for a in operands))
    next_weights, p_new, m_new, first, second = store(results)
    return (
        next_weights,
        p_new.reshape(1, 64, 128),
        m_new.reshape(1, 64, 128),
        first.reshape(1, 64, 1024),
        second.reshape(1, 64, 1024),
    )


def solution(mesh):
    return jax.shard_map(
        local,
        mesh=mesh,
        in_specs=(
            P("replica", "fsdp", "tensor", None),
            P("replica", "tensor", "fsdp"),
            P("replica", "tensor", "fsdp"),
            P("replica", "tensor", "fsdp"),
            P("replica", "tensor", "fsdp"),
            P("replica", "tensor", "fsdp"),
        ),
        out_specs=(
            P("tensor", None),
            P("replica", "tensor", "fsdp"),
            P("replica", "tensor", "fsdp"),
            P("replica", "tensor", "fsdp"),
            P("replica", "tensor", "fsdp"),
        ),
        check_vma=False,
    )
```

```python
import jax
import jax.numpy as jnp
from jax import lax
from jax.experimental import pallas as pl
from jax.experimental.pallas import tpu as pltpu
from jax.sharding import PartitionSpec as P

MESH = pl.DeviceIdType.MESH
STEP = 100
UNITS = (2, 1, 1)
CHUNKS = len(UNITS)
ORDER = (
    "S0", "S1", "S2", "N0", "L0", "R0", "R1", "R2",
    "O0", "O1", "O2", "C0", "C1", "C2", "W0", "W1",
    "W2", "F0", "F1", "F2", "Dh", "Dc", "Dr", "Dt",
)
PIECES = 2
FIRST = tuple(sum(UNITS[:c]) for c in range(len(UNITS)))

beta_first = 0.9
beta_second = 0.95
inner_rate = 0.01
weight_decay = 0.1
epsilon = 1e-08
outer_rate = 0.7
momentum_factor = 0.9

FSDP = [(2, 0), (2, 1), (1, 0), (3, 0), (1, 1), (3, 1), (0, 1)]
COLUMN = [(2, 0), (2, 1), (1, 0), (3, 0), (1, 1), (3, 1), (0, 1)]
HIGH = [2, 1, 3]
ACROSS = [2, 1, 3]


def inner_adamw(gradient, params, first_in, second_in):
    first_out = beta_first * first_in + (1.0 - beta_first) * gradient
    second_out = beta_second * second_in + (1.0 - beta_second) * gradient * gradient
    first_scale = 1.0 / (1.0 - beta_first**STEP)
    second_scale = 1.0 / (1.0 - beta_second**STEP)
    direction = first_out * first_scale / (jnp.sqrt(second_out * second_scale) + epsilon)
    updated = params - inner_rate * (direction + weight_decay * params)
    return (first_out, second_out, updated)


def nesterov(mean_params, outer_in, momentum):
    pseudo_grad = outer_in - mean_params
    momentum_new = momentum_factor * momentum + pseudo_grad
    params_new = outer_in - outer_rate * (pseudo_grad + momentum_factor * momentum_new)
    return (params_new, momentum_new)


SCALE = 2048.0
POWER = 13


def encode(weights):
    t = jnp.clip(weights * SCALE, -850.0, 850.0)
    t4 = (t * t) * (t * t)
    return (t4 * t4 * t4 * t).astype(jnp.bfloat16)


def decode(codes):
    c = codes.astype(jnp.float32)
    size = jnp.exp2(jnp.log2(jnp.maximum(jnp.abs(c), 1e-37)) * (1.0 / POWER)) * (1.0 / SCALE)
    return jnp.where(c == 0.0, 0.0, jnp.where(c < 0.0, -size, size))


def kernel(
    g_hbm, p_hbm, m1_hbm, m2_hbm, op_hbm, om_hbm,
    full, p_out, m_out, first_out, second_out,
    own, parts, params, first_in, second_in, outer_in, momentum_in,
    updated, other, pair, sums,
    near_a, near_b, local_sem, grad_send, grad_recv, core_send, core_recv, high_send, high_recv,
    col_send, col_recv, row_send, row_recv, twin_send, twin_recv,
):
    near_sems = (near_a, near_b)
    replica, f = lax.axis_index("replica"), lax.axis_index("fsdp")
    yh, core = replica // 2, lax.rem(replica, 2)
    x, yl = f // 2, lax.rem(f, 2)

    def row_band(c):
        return pl.ds(FIRST[c] * 16, UNITS[c] * 16)

    def tile_band(c):
        return pl.ds(FIRST[c] * 2, UNITS[c] * 2)

    def unit_band(c):
        return pl.ds(FIRST[c], UNITS[c])

    def at_x(step):
        return lax.rem(x + step + 4, 4)

    def at_yh(step):
        return lax.rem(yh + step + 4, 4)

    def at_yl(flip):
        return 1 - yl if flip else yl

    twin = {"replica": yh * 2 + 1 - core}

    barrier = pltpu.get_barrier_semaphore()
    peers = [{"fsdp": at_x(s) * 2 + at_yl(flip)} for s, flip in FSDP]
    peers += [{"replica": at_yh(s) * 2 + core} for s in (1, 3)]
    peers += [twin]
    for peer in peers:
        pl.semaphore_signal(barrier, inc=1, device_id=peer, device_id_type=MESH)

    mine = pl.ds(pl.multiple_of(f * 1024, 1024), 1024)
    loads = [
        pltpu.make_async_copy(src, dst, local_sem.at[i])
        for i, (src, dst) in enumerate(
            (
                (g_hbm.at[:, mine], own),
                (p_hbm, params),
                (m1_hbm, first_in),
                (m2_hbm, second_in),
                (op_hbm, outer_in),
                (om_hbm, momentum_in),
            )
        )
    ]
    for load in loads:
        load.start()
    pl.semaphore_wait(barrier, len(peers))

    def remote(src, dst, send, recv, peer):
        return pltpu.make_async_remote_copy(
            src_ref=src, dst_ref=dst, send_sem=send, recv_sem=recv, device_id=peer, device_id_type=MESH
        )

    def grad_copy(c, j):
        s, flip = FSDP[j]
        to = at_x(s) * 2 + at_yl(flip)
        band = row_band(c)
        return remote(
            g_hbm.at[band, pl.ds(pl.multiple_of(to * 1024, 1024), 1024)],
            parts.at[j, band], grad_send.at[c, j], grad_recv.at[c, j], {"fsdp": to},
        )

    def core_copy(c):
        band = tile_band(c)
        return remote(updated.at[band, :, 1 - core], other.at[band], core_send.at[c], core_recv.at[c], twin)

    def high_copy(c, j):
        band = tile_band(c)
        to = at_yh(HIGH[j])
        return remote(
            pair.at[band, to], sums.at[j, band], high_send.at[c, j], high_recv.at[c, j], {"replica": to * 2 + core}
        )

    def col_copy(c, j, arriving=False):
        s, flip = COLUMN[j]
        band = unit_band(c)
        block = full.at[band, x, at_yl(flip), at_yh(-s), core] if arriving else full.at[band, x, yl, yh, core]
        peer = {"replica": at_yh(s) * 2 + core, "fsdp": x * 2 + at_yl(flip)}
        return remote(block, block, col_send.at[c, j], col_recv.at[c, j], peer)

    def row_copy(c, j, half, arriving=False):
        block = full.at[unit_band(c), at_x(-ACROSS[j]) if arriving else x, at_yl(half), :, core]
        k = j + 3 * half
        return remote(block, block, row_send.at[c, k], row_recv.at[c, k], {"fsdp": at_x(ACROSS[j]) * 2 + yl})

    def twin_copy(c, arriving=False):
        block = full.at[unit_band(c), :, :, :, 1 - core if arriving else core]
        return remote(block, block, twin_send.at[c], twin_recv.at[c], twin)

    def send_gradient(c):
        for j in range(7):
            grad_copy(c, j).start()

    def reduce_gradient(c):
        for j in range(7):
            grad_copy(c, j).wait_recv()
        for u in range(FIRST[c], FIRST[c] + UNITS[c]):
            band = pl.ds(u * 16, 16)
            for q in range(4):
                cols = pl.ds(q * 256, 256)
                gradient = own[band, cols].astype(jnp.float32)
                for j in range(7):
                    gradient = gradient + parts[j, band, cols].astype(jnp.float32)
                first, second, new = inner_adamw(
                    gradient, params[band, cols], first_in[band, cols], second_in[band, cols]
                )
                first_out[band, cols] = first
                second_out[band, cols] = second
                for t in range(2):
                    for h in range(2):
                        updated[2 * u + t, q, h] = new[t * 8 : t * 8 + 8, h * 128 : h * 128 + 128]
        core_copy(c).start()
        core_copy(c).wait_recv()
        band = tile_band(c)
        pair[band] = updated[band, :, core] + other[band]
        for j in range(3):
            high_copy(c, j).start()

    def outer_step(c):
        for j in range(3):
            high_copy(c, j).wait_recv()
        band = tile_band(c)
        total = pair[band, yh] + sums[0, band] + sums[1, band] + sums[2, band]
        new, momentum = nesterov(total * 0.125, outer_in[band], momentum_in[band])
        p_out[band] = new
        m_out[band] = momentum
        full[unit_band(c), x, yl, yh, core] = encode(new.reshape(UNITS[c], 16, 128))
        for j in range(7):
            col_copy(c, j).start()

    def to_rows(c):
        for half in (1, 0):
            for j in range(7):
                if COLUMN[j][1] == half:
                    col_copy(c, j, True).wait_recv()
            for j in range(3):
                row_copy(c, j, half).start()

    def to_twin(c):
        for j in (1, 2, 0):
            for half in (1, 0):
                row_copy(c, j, half, True).wait_recv()
        twin_copy(c).start()

    def finish(c):
        twin_copy(c, True).wait_recv()

    def ready(c):
        for sem in near_sems:
            for step in (1, 3):
                pl.semaphore_signal(
                    sem, inc=1, device_id={"replica": at_yh(step) * 2 + core}, device_id_type=MESH
                )
            pl.semaphore_wait(sem, 2)

    def loaded(c):
        for load in loads:
            load.wait()

    stages = {"S": send_gradient, "N": ready, "L": loaded, "R": reduce_gradient, "O": outer_step, "C": to_rows, "W": to_twin, "F": finish}
    def drain(kind):
        for c in range(CHUNKS):
            if kind == "h":
                for j in range(7):
                    grad_copy(c, j).wait_send()
                core_copy(c).wait_send()
                for j in range(3):
                    high_copy(c, j).wait_send()
            elif kind == "c":
                for j in range(7):
                    col_copy(c, j).wait_send()
            elif kind == "r":
                for j in range(3):
                    row_copy(c, j, 0).wait_send()
                    row_copy(c, j, 1).wait_send()
            else:
                twin_copy(c).wait_send()

    for step in ORDER:
        if step[0] == "D":
            drain(step[1])
        else:
            stages[step[0]](int(step[1]))


def store_kernel(*refs):
    sources, targets, weights, sems = refs[:5], refs[5:10], refs[10], refs[11]
    codes = sources[0]
    copies = [pltpu.make_async_copy(sources[i], targets[i], sems.at[i]) for i in range(1, 5)]
    for copy in copies:
        copy.start()
    for c in range(4):
        band = pl.ds(c * 16, 16)

        for p in range(PIECES):
            for x in range(p * (4 // PIECES), (p + 1) * (4 // PIECES)):
                for yl in range(2):
                    for yh in range(4):
                        for core in range(2):
                            at = x * 2048 + yl * 1024 + yh * 256 + core * 128
                            weights[band, pl.ds(at, 128)] = decode(codes[c, x, yl, yh, core])
            part = pl.ds(p * (8192 // PIECES), 8192 // PIECES)
            copy = pltpu.make_async_copy(weights.at[band, part], targets[0].at[band, part], sems.at[5 + c * PIECES + p])
            copy.start()
            copies.append(copy)
    for copy in copies:
        copy.wait()


def store(arrays):
    shapes = [(64, 8192)] + [a.shape for a in arrays[1:]]
    return pl.pallas_call(
        store_kernel,
        out_shape=tuple(jax.ShapeDtypeStruct(shape, jnp.float32) for shape in shapes),
        in_specs=[pl.BlockSpec(memory_space=pltpu.VMEM)] * 5,
        out_specs=(pl.BlockSpec(memory_space=pltpu.HBM),) * 5,
        scratch_shapes=[pltpu.VMEM((64, 8192), jnp.float32), pltpu.SemaphoreType.DMA((5 + 4 * PIECES,))],
        name="store",
    )(*(pltpu.with_memory_space_constraint(a, pltpu.VMEM) for a in arrays))


def local(grad_parts, inner_params, first_moment, second_moment, outer_params, outer_momentum):
    f32, bf16 = jnp.float32, jnp.bfloat16
    dma = pltpu.SemaphoreType.DMA
    vmem = pl.BlockSpec(memory_space=pltpu.VMEM)
    operands = (
        grad_parts.reshape(64, 8192),
        inner_params.reshape(64, 1024),
        first_moment.reshape(64, 1024),
        second_moment.reshape(64, 1024),
        outer_params.reshape(8, 8, 128),
        outer_momentum.reshape(8, 8, 128),
    )
    results = pl.pallas_call(
        kernel,
        out_shape=(
            pltpu.VMEM((4, 4, 2, 4, 2, 16, 128), bf16),
            pltpu.VMEM((8, 8, 128), f32),
            pltpu.VMEM((8, 8, 128), f32),
            pltpu.VMEM((64, 1024), f32),
            pltpu.VMEM((64, 1024), f32),
        ),
        in_specs=[pl.BlockSpec(memory_space=pltpu.HBM)] * 6,
        out_specs=(vmem,) * 5,
        scratch_shapes=[
            pltpu.VMEM((64, 1024), bf16),
            pltpu.VMEM((7, 64, 1024), bf16),
            pltpu.VMEM((64, 1024), f32),
            pltpu.VMEM((64, 1024), f32),
            pltpu.VMEM((64, 1024), f32),
            pltpu.VMEM((8, 8, 128), f32),
            pltpu.VMEM((8, 8, 128), f32),
            pltpu.VMEM((8, 4, 2, 8, 128), f32),
            pltpu.VMEM((8, 4, 8, 128), f32),
            pltpu.VMEM((8, 4, 8, 128), f32),
            pltpu.VMEM((3, 8, 8, 128), f32),
            pltpu.SemaphoreType.REGULAR,
            pltpu.SemaphoreType.REGULAR,
            dma((6,)),
            dma((CHUNKS, 7)), dma((CHUNKS, 7)),
            dma((CHUNKS,)), dma((CHUNKS,)),
            dma((CHUNKS, 3)), dma((CHUNKS, 3)),
            dma((CHUNKS, 7)), dma((CHUNKS, 7)),
            dma((CHUNKS, 6)), dma((CHUNKS, 6)),
            dma((CHUNKS,)), dma((CHUNKS,)),
        ],
        compiler_params=pltpu.CompilerParams(
            collective_id=0, has_side_effects=True, vmem_limit_bytes=32 * 2**20
        ),
        name="sync",
    )(*(pltpu.with_memory_space_constraint(a, pltpu.HBM) for a in operands))
    next_weights, p_new, m_new, first, second = store(results)
    return (
        next_weights,
        p_new.reshape(1, 64, 128),
        m_new.reshape(1, 64, 128),
        first.reshape(1, 64, 1024),
        second.reshape(1, 64, 1024),
    )


def solution(mesh):
    return jax.shard_map(
        local,
        mesh=mesh,
        in_specs=(
            P("replica", "fsdp", "tensor", None),
            P("replica", "tensor", "fsdp"),
            P("replica", "tensor", "fsdp"),
            P("replica", "tensor", "fsdp"),
            P("replica", "tensor", "fsdp"),
            P("replica", "tensor", "fsdp"),
        ),
        out_specs=(
            P("tensor", None),
            P("replica", "tensor", "fsdp"),
            P("replica", "tensor", "fsdp"),
            P("replica", "tensor", "fsdp"),
            P("replica", "tensor", "fsdp"),
        ),
        check_vma=False,
    )
```

```python
import jax
import jax.numpy as jnp
from jax import lax
from jax.experimental import pallas as pl
from jax.experimental.pallas import tpu as pltpu
from jax.sharding import PartitionSpec as P

MESH = pl.DeviceIdType.MESH
STEP = 100
UNITS = (2, 1, 1)
CHUNKS = len(UNITS)
ORDER = (
    "S0", "S1", "S2", "N0", "L0", "R0", "R1", "R2",
    "O0", "O1", "O2", "C0", "C1", "C2", "W0", "W1",
    "W2", "F0", "F1", "F2", "Dh", "Dc", "Dr", "Dt",
)
PIECES = 2
FIRST = tuple(sum(UNITS[:c]) for c in range(len(UNITS)))

beta_first = 0.9
beta_second = 0.95
inner_rate = 0.01
weight_decay = 0.1
epsilon = 1e-08
outer_rate = 0.7
momentum_factor = 0.9

FSDP = [(2, 0), (2, 1), (1, 0), (3, 0), (1, 1), (3, 1), (0, 1)]
COLUMN = [(2, 0), (2, 1), (1, 0), (3, 0), (1, 1), (3, 1), (0, 1)]
HIGH = [2, 1, 3]
ACROSS = [2, 1, 3]


def inner_adamw(gradient, params, first_in, second_in):
    first_out = beta_first * first_in + (1.0 - beta_first) * gradient
    second_out = beta_second * second_in + (1.0 - beta_second) * gradient * gradient
    first_scale = 1.0 / (1.0 - beta_first**STEP)
    second_scale = 1.0 / (1.0 - beta_second**STEP)
    direction = first_out * first_scale / (jnp.sqrt(second_out * second_scale) + epsilon)
    updated = params - inner_rate * (direction + weight_decay * params)
    return (first_out, second_out, updated)


def nesterov(mean_params, outer_in, momentum):
    pseudo_grad = outer_in - mean_params
    momentum_new = momentum_factor * momentum + pseudo_grad
    params_new = outer_in - outer_rate * (pseudo_grad + momentum_factor * momentum_new)
    return (params_new, momentum_new)


SCALE = 2048.0
POWER = 13


def encode(weights):
    t = jnp.clip(weights * SCALE, -850.0, 850.0)
    t4 = (t * t) * (t * t)
    return (t4 * t4 * t4 * t).astype(jnp.bfloat16)


def decode(codes):
    c = codes.astype(jnp.float32)
    size = jnp.exp2(jnp.log2(jnp.maximum(jnp.abs(c), 1e-37)) * (1.0 / POWER)) * (1.0 / SCALE)
    return jnp.where(c == 0.0, 0.0, jnp.where(c < 0.0, -size, size))


def kernel(
    g_hbm, p_hbm, m1_hbm, m2_hbm, op_hbm, om_hbm,
    full, p_out, m_out, first_out, second_out,
    own, parts, params, first_in, second_in, outer_in, momentum_in,
    updated, other, pair, sums,
    near_a, near_b, local_sem, grad_send, grad_recv, core_send, core_recv, high_send, high_recv,
    col_send, col_recv, row_send, row_recv, twin_send, twin_recv,
):
    near_sems = (near_a, near_b)
    replica, f = lax.axis_index("replica"), lax.axis_index("fsdp")
    yh, core = replica // 2, lax.rem(replica, 2)
    x, yl = f // 2, lax.rem(f, 2)

    def tile_band(c):
        return pl.ds(FIRST[c] * 2, UNITS[c] * 2)

    def unit_band(c):
        return pl.ds(FIRST[c], UNITS[c])

    def at_x(step):
        return lax.rem(x + step + 4, 4)

    def at_yh(step):
        return lax.rem(yh + step + 4, 4)

    def at_yl(flip):
        return 1 - yl if flip else yl

    twin = {"replica": yh * 2 + 1 - core}

    barrier = pltpu.get_barrier_semaphore()
    peers = [{"fsdp": at_x(s) * 2 + at_yl(flip)} for s, flip in FSDP]
    peers += [{"replica": at_yh(s) * 2 + core} for s in (1, 3)]
    peers += [twin]
    for peer in peers:
        pl.semaphore_signal(barrier, inc=1, device_id=peer, device_id_type=MESH)

    mine = pl.ds(pl.multiple_of(f * 1024, 1024), 1024)
    loads = [
        pltpu.make_async_copy(src, dst, local_sem.at[i])
        for i, (src, dst) in enumerate(
            (
                (g_hbm.at[:, mine], own),
                (p_hbm, params),
                (m1_hbm, first_in),
                (m2_hbm, second_in),
                (op_hbm, outer_in),
                (om_hbm, momentum_in),
            )
        )
    ]
    for load in loads:
        load.start()
    pl.semaphore_wait(barrier, len(peers))

    def remote(src, dst, send, recv, peer):
        return pltpu.make_async_remote_copy(
            src_ref=src, dst_ref=dst, send_sem=send, recv_sem=recv, device_id=peer, device_id_type=MESH
        )

    def grad_copy(c, j):
        s, flip = FSDP[j]
        to = at_x(s) * 2 + at_yl(flip)
        band = pl.ds(c * 16, 16)
        return remote(
            g_hbm.at[band, pl.ds(pl.multiple_of(to * 1024, 1024), 1024)],
            parts.at[j, band], grad_send.at[c, j], grad_recv.at[c, j], {"fsdp": to},
        )

    def core_copy(c):
        band = tile_band(c)
        return remote(updated.at[band, :, 1 - core], other.at[band], core_send.at[c], core_recv.at[c], twin)

    def high_copy(c, j):
        band = tile_band(c)
        to = at_yh(HIGH[j])
        return remote(
            pair.at[band, to], sums.at[j, band], high_send.at[c, j], high_recv.at[c, j], {"replica": to * 2 + core}
        )

    def col_copy(c, j, arriving=False):
        s, flip = COLUMN[j]
        band = unit_band(c)
        block = full.at[band, x, at_yl(flip), at_yh(-s), core] if arriving else full.at[band, x, yl, yh, core]
        peer = {"replica": at_yh(s) * 2 + core, "fsdp": x * 2 + at_yl(flip)}
        return remote(block, block, col_send.at[c, j], col_recv.at[c, j], peer)

    def row_copy(c, j, half, arriving=False):
        block = full.at[unit_band(c), at_x(-ACROSS[j]) if arriving else x, at_yl(half), :, core]
        k = j + 3 * half
        return remote(block, block, row_send.at[c, k], row_recv.at[c, k], {"fsdp": at_x(ACROSS[j]) * 2 + yl})

    def twin_copy(c, arriving=False):
        block = full.at[unit_band(c), :, :, :, 1 - core if arriving else core]
        return remote(block, block, twin_send.at[c], twin_recv.at[c], twin)

    def send_gradient(c):
        for u in range(FIRST[c], FIRST[c] + UNITS[c]):
            for j in range(7):
                grad_copy(u, j).start()

    def reduce_gradient(c):
        for u in range(FIRST[c], FIRST[c] + UNITS[c]):
            for j in range(7):
                grad_copy(u, j).wait_recv()
            band = pl.ds(u * 16, 16)
            for q in range(4):
                cols = pl.ds(q * 256, 256)
                gradient = own[band, cols].astype(jnp.float32)
                for j in range(7):
                    gradient = gradient + parts[j, band, cols].astype(jnp.float32)
                first, second, new = inner_adamw(
                    gradient, params[band, cols], first_in[band, cols], second_in[band, cols]
                )
                first_out[band, cols] = first
                second_out[band, cols] = second
                for t in range(2):
                    for h in range(2):
                        updated[2 * u + t, q, h] = new[t * 8 : t * 8 + 8, h * 128 : h * 128 + 128]
        core_copy(c).start()
        core_copy(c).wait_recv()
        band = tile_band(c)
        pair[band] = updated[band, :, core] + other[band]
        for j in range(3):
            high_copy(c, j).start()

    def outer_step(c):
        for j in range(3):
            high_copy(c, j).wait_recv()
        band = tile_band(c)
        total = pair[band, yh] + sums[0, band] + sums[1, band] + sums[2, band]
        new, momentum = nesterov(total * 0.125, outer_in[band], momentum_in[band])
        p_out[band] = new
        m_out[band] = momentum
        full[unit_band(c), x, yl, yh, core] = encode(new.reshape(UNITS[c], 16, 128))
        for j in range(7):
            col_copy(c, j).start()

    def to_rows(c):
        for half in (1, 0):
            for j in range(7):
                if COLUMN[j][1] == half:
                    col_copy(c, j, True).wait_recv()
            for j in range(3):
                row_copy(c, j, half).start()

    def to_twin(c):
        for j in (1, 2, 0):
            for half in (1, 0):
                row_copy(c, j, half, True).wait_recv()
        twin_copy(c).start()

    def finish(c):
        twin_copy(c, True).wait_recv()

    def ready(c):
        for sem in near_sems:
            for step in (1, 3):
                pl.semaphore_signal(
                    sem, inc=1, device_id={"replica": at_yh(step) * 2 + core}, device_id_type=MESH
                )
            pl.semaphore_wait(sem, 2)

    def loaded(c):
        for load in loads:
            load.wait()

    stages = {"S": send_gradient, "N": ready, "L": loaded, "R": reduce_gradient, "O": outer_step, "C": to_rows, "W": to_twin, "F": finish}
    def drain(kind):
        for c in range(CHUNKS):
            if kind == "h":
                for u in range(FIRST[c], FIRST[c] + UNITS[c]):
                    for j in range(7):
                        grad_copy(u, j).wait_send()
                core_copy(c).wait_send()
                for j in range(3):
                    high_copy(c, j).wait_send()
            elif kind == "c":
                for j in range(7):
                    col_copy(c, j).wait_send()
            elif kind == "r":
                for j in range(3):
                    row_copy(c, j, 0).wait_send()
                    row_copy(c, j, 1).wait_send()
            else:
                twin_copy(c).wait_send()

    for step in ORDER:
        if step[0] == "D":
            drain(step[1])
        else:
            stages[step[0]](int(step[1]))


def store_kernel(*refs):
    sources, targets, weights, sems = refs[:5], refs[5:10], refs[10], refs[11]
    codes = sources[0]
    copies = [pltpu.make_async_copy(sources[i], targets[i], sems.at[i]) for i in range(1, 5)]
    for copy in copies:
        copy.start()
    for c in range(4):
        band = pl.ds(c * 16, 16)

        for p in range(PIECES):
            for x in range(p * (4 // PIECES), (p + 1) * (4 // PIECES)):
                for yl in range(2):
                    for yh in range(4):
                        for core in range(2):
                            at = x * 2048 + yl * 1024 + yh * 256 + core * 128
                            weights[band, pl.ds(at, 128)] = decode(codes[c, x, yl, yh, core])
            part = pl.ds(p * (8192 // PIECES), 8192 // PIECES)
            copy = pltpu.make_async_copy(weights.at[band, part], targets[0].at[band, part], sems.at[5 + c * PIECES + p])
            copy.start()
            copies.append(copy)
    for copy in copies:
        copy.wait()


def store(arrays):
    shapes = [(64, 8192)] + [a.shape for a in arrays[1:]]
    return pl.pallas_call(
        store_kernel,
        out_shape=tuple(jax.ShapeDtypeStruct(shape, jnp.float32) for shape in shapes),
        in_specs=[pl.BlockSpec(memory_space=pltpu.VMEM)] * 5,
        out_specs=(pl.BlockSpec(memory_space=pltpu.HBM),) * 5,
        scratch_shapes=[pltpu.VMEM((64, 8192), jnp.float32), pltpu.SemaphoreType.DMA((5 + 4 * PIECES,))],
        name="store",
    )(*(pltpu.with_memory_space_constraint(a, pltpu.VMEM) for a in arrays))


def local(grad_parts, inner_params, first_moment, second_moment, outer_params, outer_momentum):
    f32, bf16 = jnp.float32, jnp.bfloat16
    dma = pltpu.SemaphoreType.DMA
    vmem = pl.BlockSpec(memory_space=pltpu.VMEM)
    operands = (
        grad_parts.reshape(64, 8192),
        inner_params.reshape(64, 1024),
        first_moment.reshape(64, 1024),
        second_moment.reshape(64, 1024),
        outer_params.reshape(8, 8, 128),
        outer_momentum.reshape(8, 8, 128),
    )
    results = pl.pallas_call(
        kernel,
        out_shape=(
            pltpu.VMEM((4, 4, 2, 4, 2, 16, 128), bf16),
            pltpu.VMEM((8, 8, 128), f32),
            pltpu.VMEM((8, 8, 128), f32),
            pltpu.VMEM((64, 1024), f32),
            pltpu.VMEM((64, 1024), f32),
        ),
        in_specs=[pl.BlockSpec(memory_space=pltpu.HBM)] * 6,
        out_specs=(vmem,) * 5,
        scratch_shapes=[
            pltpu.VMEM((64, 1024), bf16),
            pltpu.VMEM((7, 64, 1024), bf16),
            pltpu.VMEM((64, 1024), f32),
            pltpu.VMEM((64, 1024), f32),
            pltpu.VMEM((64, 1024), f32),
            pltpu.VMEM((8, 8, 128), f32),
            pltpu.VMEM((8, 8, 128), f32),
            pltpu.VMEM((8, 4, 2, 8, 128), f32),
            pltpu.VMEM((8, 4, 8, 128), f32),
            pltpu.VMEM((8, 4, 8, 128), f32),
            pltpu.VMEM((3, 8, 8, 128), f32),
            pltpu.SemaphoreType.REGULAR,
            pltpu.SemaphoreType.REGULAR,
            dma((6,)),
            dma((4, 7)), dma((4, 7)),
            dma((CHUNKS,)), dma((CHUNKS,)),
            dma((CHUNKS, 3)), dma((CHUNKS, 3)),
            dma((CHUNKS, 7)), dma((CHUNKS, 7)),
            dma((CHUNKS, 6)), dma((CHUNKS, 6)),
            dma((CHUNKS,)), dma((CHUNKS,)),
        ],
        compiler_params=pltpu.CompilerParams(
            collective_id=0, has_side_effects=True, vmem_limit_bytes=32 * 2**20
        ),
        name="sync",
    )(*(pltpu.with_memory_space_constraint(a, pltpu.HBM) for a in operands))
    next_weights, p_new, m_new, first, second = store(results)
    return (
        next_weights,
        p_new.reshape(1, 64, 128),
        m_new.reshape(1, 64, 128),
        first.reshape(1, 64, 1024),
        second.reshape(1, 64, 1024),
    )


def solution(mesh):
    return jax.shard_map(
        local,
        mesh=mesh,
        in_specs=(
            P("replica", "fsdp", "tensor", None),
            P("replica", "tensor", "fsdp"),
            P("replica", "tensor", "fsdp"),
            P("replica", "tensor", "fsdp"),
            P("replica", "tensor", "fsdp"),
            P("replica", "tensor", "fsdp"),
        ),
        out_specs=(
            P("tensor", None),
            P("replica", "tensor", "fsdp"),
            P("replica", "tensor", "fsdp"),
            P("replica", "tensor", "fsdp"),
            P("replica", "tensor", "fsdp"),
        ),
        check_vma=False,
    )
```

```python
import jax
import jax.numpy as jnp
from jax import lax
from jax.experimental import pallas as pl
from jax.experimental.pallas import tpu as pltpu
from jax.sharding import PartitionSpec as P

MESH = pl.DeviceIdType.MESH
STEP = 100
UNITS = (2, 1, 1)
CHUNKS = len(UNITS)
ORDER = (
    "S0", "S1", "S2", "N0", "L0", "R0", "X0", "R1", "R2", "X1", "X2",
    "O0", "O1", "O2", "C0", "C1", "C2", "W0", "W1",
    "W2", "F0", "F1", "F2", "Dh", "Dc", "Dr", "Dt",
)
PIECES = 2
FIRST = tuple(sum(UNITS[:c]) for c in range(len(UNITS)))

beta_first = 0.9
beta_second = 0.95
inner_rate = 0.01
weight_decay = 0.1
epsilon = 1e-08
outer_rate = 0.7
momentum_factor = 0.9

FSDP = [(2, 0), (2, 1), (1, 0), (3, 0), (1, 1), (3, 1), (0, 1)]
COLUMN = [(2, 0), (2, 1), (1, 0), (3, 0), (1, 1), (3, 1), (0, 1)]
HIGH = [2, 1, 3]
ACROSS = [2, 1, 3]


def inner_adamw(gradient, params, first_in, second_in):
    first_out = beta_first * first_in + (1.0 - beta_first) * gradient
    second_out = beta_second * second_in + (1.0 - beta_second) * gradient * gradient
    first_scale = 1.0 / (1.0 - beta_first**STEP)
    second_scale = 1.0 / (1.0 - beta_second**STEP)
    direction = first_out * first_scale / (jnp.sqrt(second_out * second_scale) + epsilon)
    updated = params - inner_rate * (direction + weight_decay * params)
    return (first_out, second_out, updated)


def nesterov(mean_params, outer_in, momentum):
    pseudo_grad = outer_in - mean_params
    momentum_new = momentum_factor * momentum + pseudo_grad
    params_new = outer_in - outer_rate * (pseudo_grad + momentum_factor * momentum_new)
    return (params_new, momentum_new)


SCALE = 2048.0
POWER = 13


def encode(weights):
    t = jnp.clip(weights * SCALE, -850.0, 850.0)
    t4 = (t * t) * (t * t)
    return (t4 * t4 * t4 * t).astype(jnp.bfloat16)


def decode(codes):
    c = codes.astype(jnp.float32)
    size = jnp.exp2(jnp.log2(jnp.maximum(jnp.abs(c), 1e-37)) * (1.0 / POWER)) * (1.0 / SCALE)
    return jnp.where(c == 0.0, 0.0, jnp.where(c < 0.0, -size, size))


def kernel(
    g_hbm, p_hbm, m1_hbm, m2_hbm, op_hbm, om_hbm,
    full, p_out, m_out, first_out, second_out,
    own, parts, params, first_in, second_in, outer_in, momentum_in,
    updated, other, pair, sums,
    near_a, near_b, local_sem, grad_send, grad_recv, core_send, core_recv, high_send, high_recv,
    col_send, col_recv, row_send, row_recv, twin_send, twin_recv,
):
    near_sems = (near_a, near_b)
    replica, f = lax.axis_index("replica"), lax.axis_index("fsdp")
    yh, core = replica // 2, lax.rem(replica, 2)
    x, yl = f // 2, lax.rem(f, 2)

    def row_band(c):
        return pl.ds(FIRST[c] * 16, UNITS[c] * 16)

    def tile_band(c):
        return pl.ds(FIRST[c] * 2, UNITS[c] * 2)

    def unit_band(c):
        return pl.ds(FIRST[c], UNITS[c])

    def at_x(step):
        return lax.rem(x + step + 4, 4)

    def at_yh(step):
        return lax.rem(yh + step + 4, 4)

    def at_yl(flip):
        return 1 - yl if flip else yl

    twin = {"replica": yh * 2 + 1 - core}

    barrier = pltpu.get_barrier_semaphore()
    peers = [{"fsdp": at_x(s) * 2 + at_yl(flip)} for s, flip in FSDP]
    peers += [{"replica": at_yh(s) * 2 + core} for s in (1, 3)]
    peers += [twin]
    for peer in peers:
        pl.semaphore_signal(barrier, inc=1, device_id=peer, device_id_type=MESH)

    mine = pl.ds(pl.multiple_of(f * 1024, 1024), 1024)
    loads = [
        pltpu.make_async_copy(src, dst, local_sem.at[i])
        for i, (src, dst) in enumerate(
            (
                (g_hbm.at[:, mine], own),
                (p_hbm, params),
                (m1_hbm, first_in),
                (m2_hbm, second_in),
                (op_hbm, outer_in),
                (om_hbm, momentum_in),
            )
        )
    ]
    for load in loads:
        load.start()
    pl.semaphore_wait(barrier, len(peers))

    def remote(src, dst, send, recv, peer):
        return pltpu.make_async_remote_copy(
            src_ref=src, dst_ref=dst, send_sem=send, recv_sem=recv, device_id=peer, device_id_type=MESH
        )

    def grad_copy(c, j):
        s, flip = FSDP[j]
        to = at_x(s) * 2 + at_yl(flip)
        band = row_band(c)
        return remote(
            g_hbm.at[band, pl.ds(pl.multiple_of(to * 1024, 1024), 1024)],
            parts.at[j, band], grad_send.at[c, j], grad_recv.at[c, j], {"fsdp": to},
        )

    def core_copy(c):
        band = tile_band(c)
        return remote(updated.at[band, :, 1 - core], other.at[band], core_send.at[c], core_recv.at[c], twin)

    def high_copy(c, j):
        band = tile_band(c)
        to = at_yh(HIGH[j])
        return remote(
            pair.at[band, to], sums.at[j, band], high_send.at[c, j], high_recv.at[c, j], {"replica": to * 2 + core}
        )

    def col_copy(c, j, arriving=False):
        s, flip = COLUMN[j]
        band = unit_band(c)
        block = full.at[band, x, at_yl(flip), at_yh(-s), core] if arriving else full.at[band, x, yl, yh, core]
        peer = {"replica": at_yh(s) * 2 + core, "fsdp": x * 2 + at_yl(flip)}
        return remote(block, block, col_send.at[c, j], col_recv.at[c, j], peer)

    def row_copy(c, j, half, arriving=False):
        block = full.at[unit_band(c), at_x(-ACROSS[j]) if arriving else x, at_yl(half), :, core]
        k = j + 3 * half
        return remote(block, block, row_send.at[c, k], row_recv.at[c, k], {"fsdp": at_x(ACROSS[j]) * 2 + yl})

    def twin_copy(c, arriving=False):
        block = full.at[unit_band(c), :, :, :, 1 - core if arriving else core]
        return remote(block, block, twin_send.at[c], twin_recv.at[c], twin)

    def send_gradient(c):
        for j in range(7):
            grad_copy(c, j).start()

    def reduce_gradient(c):
        for j in range(7):
            grad_copy(c, j).wait_recv()
        for u in range(FIRST[c], FIRST[c] + UNITS[c]):
            band = pl.ds(u * 16, 16)
            for q in range(4):
                cols = pl.ds(q * 256, 256)
                gradient = own[band, cols].astype(jnp.float32)
                for j in range(7):
                    gradient = gradient + parts[j, band, cols].astype(jnp.float32)
                first, second, new = inner_adamw(
                    gradient, params[band, cols], first_in[band, cols], second_in[band, cols]
                )
                first_out[band, cols] = first
                second_out[band, cols] = second
                for t in range(2):
                    for h in range(2):
                        updated[2 * u + t, q, h] = new[t * 8 : t * 8 + 8, h * 128 : h * 128 + 128]
        core_copy(c).start()

    def sum_cores(c):
        core_copy(c).wait_recv()
        band = tile_band(c)
        pair[band] = updated[band, :, core] + other[band]
        for j in range(3):
            high_copy(c, j).start()

    def outer_step(c):
        for j in range(3):
            high_copy(c, j).wait_recv()
        band = tile_band(c)
        total = pair[band, yh] + sums[0, band] + sums[1, band] + sums[2, band]
        new, momentum = nesterov(total * 0.125, outer_in[band], momentum_in[band])
        p_out[band] = new
        m_out[band] = momentum
        full[unit_band(c), x, yl, yh, core] = encode(new.reshape(UNITS[c], 16, 128))
        for j in range(7):
            col_copy(c, j).start()

    def to_rows(c):
        for half in (1, 0):
            for j in range(7):
                if COLUMN[j][1] == half:
                    col_copy(c, j, True).wait_recv()
            for j in range(3):
                row_copy(c, j, half).start()

    def to_twin(c):
        for j in (1, 2, 0):
            for half in (1, 0):
                row_copy(c, j, half, True).wait_recv()
        twin_copy(c).start()

    def finish(c):
        twin_copy(c, True).wait_recv()

    def ready(c):
        for sem in near_sems:
            for step in (1, 3):
                pl.semaphore_signal(
                    sem, inc=1, device_id={"replica": at_yh(step) * 2 + core}, device_id_type=MESH
                )
            pl.semaphore_wait(sem, 2)

    def loaded(c):
        for load in loads:
            load.wait()

    stages = {"S": send_gradient, "N": ready, "L": loaded, "X": sum_cores, "R": reduce_gradient, "O": outer_step, "C": to_rows, "W": to_twin, "F": finish}
    def drain(kind):
        for c in range(CHUNKS):
            if kind == "h":
                for j in range(7):
                    grad_copy(c, j).wait_send()
                core_copy(c).wait_send()
                for j in range(3):
                    high_copy(c, j).wait_send()
            elif kind == "c":
                for j in range(7):
                    col_copy(c, j).wait_send()
            elif kind == "r":
                for j in range(3):
                    row_copy(c, j, 0).wait_send()
                    row_copy(c, j, 1).wait_send()
            else:
                twin_copy(c).wait_send()

    for step in ORDER:
        if step[0] == "D":
            drain(step[1])
        else:
            stages[step[0]](int(step[1]))


def store_kernel(*refs):
    sources, targets, weights, sems = refs[:5], refs[5:10], refs[10], refs[11]
    codes = sources[0]
    copies = [pltpu.make_async_copy(sources[i], targets[i], sems.at[i]) for i in range(1, 5)]
    for copy in copies:
        copy.start()
    for c in range(4):
        band = pl.ds(c * 16, 16)

        for p in range(PIECES):
            for x in range(p * (4 // PIECES), (p + 1) * (4 // PIECES)):
                for yl in range(2):
                    for yh in range(4):
                        for core in range(2):
                            at = x * 2048 + yl * 1024 + yh * 256 + core * 128
                            weights[band, pl.ds(at, 128)] = decode(codes[c, x, yl, yh, core])
            part = pl.ds(p * (8192 // PIECES), 8192 // PIECES)
            copy = pltpu.make_async_copy(weights.at[band, part], targets[0].at[band, part], sems.at[5 + c * PIECES + p])
            copy.start()
            copies.append(copy)
    for copy in copies:
        copy.wait()


def store(arrays):
    shapes = [(64, 8192)] + [a.shape for a in arrays[1:]]
    return pl.pallas_call(
        store_kernel,
        out_shape=tuple(jax.ShapeDtypeStruct(shape, jnp.float32) for shape in shapes),
        in_specs=[pl.BlockSpec(memory_space=pltpu.VMEM)] * 5,
        out_specs=(pl.BlockSpec(memory_space=pltpu.HBM),) * 5,
        scratch_shapes=[pltpu.VMEM((64, 8192), jnp.float32), pltpu.SemaphoreType.DMA((5 + 4 * PIECES,))],
        name="store",
    )(*(pltpu.with_memory_space_constraint(a, pltpu.VMEM) for a in arrays))


def local(grad_parts, inner_params, first_moment, second_moment, outer_params, outer_momentum):
    f32, bf16 = jnp.float32, jnp.bfloat16
    dma = pltpu.SemaphoreType.DMA
    vmem = pl.BlockSpec(memory_space=pltpu.VMEM)
    operands = (
        grad_parts.reshape(64, 8192),
        inner_params.reshape(64, 1024),
        first_moment.reshape(64, 1024),
        second_moment.reshape(64, 1024),
        outer_params.reshape(8, 8, 128),
        outer_momentum.reshape(8, 8, 128),
    )
    results = pl.pallas_call(
        kernel,
        out_shape=(
            pltpu.VMEM((4, 4, 2, 4, 2, 16, 128), bf16),
            pltpu.VMEM((8, 8, 128), f32),
            pltpu.VMEM((8, 8, 128), f32),
            pltpu.VMEM((64, 1024), f32),
            pltpu.VMEM((64, 1024), f32),
        ),
        in_specs=[pl.BlockSpec(memory_space=pltpu.HBM)] * 6,
        out_specs=(vmem,) * 5,
        scratch_shapes=[
            pltpu.VMEM((64, 1024), bf16),
            pltpu.VMEM((7, 64, 1024), bf16),
            pltpu.VMEM((64, 1024), f32),
            pltpu.VMEM((64, 1024), f32),
            pltpu.VMEM((64, 1024), f32),
            pltpu.VMEM((8, 8, 128), f32),
            pltpu.VMEM((8, 8, 128), f32),
            pltpu.VMEM((8, 4, 2, 8, 128), f32),
            pltpu.VMEM((8, 4, 8, 128), f32),
            pltpu.VMEM((8, 4, 8, 128), f32),
            pltpu.VMEM((3, 8, 8, 128), f32),
            pltpu.SemaphoreType.REGULAR,
            pltpu.SemaphoreType.REGULAR,
            dma((6,)),
            dma((CHUNKS, 7)), dma((CHUNKS, 7)),
            dma((CHUNKS,)), dma((CHUNKS,)),
            dma((CHUNKS, 3)), dma((CHUNKS, 3)),
            dma((CHUNKS, 7)), dma((CHUNKS, 7)),
            dma((CHUNKS, 6)), dma((CHUNKS, 6)),
            dma((CHUNKS,)), dma((CHUNKS,)),
        ],
        compiler_params=pltpu.CompilerParams(
            collective_id=0, has_side_effects=True, vmem_limit_bytes=32 * 2**20
        ),
        name="sync",
    )(*(pltpu.with_memory_space_constraint(a, pltpu.HBM) for a in operands))
    next_weights, p_new, m_new, first, second = store(results)
    return (
        next_weights,
        p_new.reshape(1, 64, 128),
        m_new.reshape(1, 64, 128),
        first.reshape(1, 64, 1024),
        second.reshape(1, 64, 1024),
    )


def solution(mesh):
    return jax.shard_map(
        local,
        mesh=mesh,
        in_specs=(
            P("replica", "fsdp", "tensor", None),
            P("replica", "tensor", "fsdp"),
            P("replica", "tensor", "fsdp"),
            P("replica", "tensor", "fsdp"),
            P("replica", "tensor", "fsdp"),
            P("replica", "tensor", "fsdp"),
        ),
        out_specs=(
            P("tensor", None),
            P("replica", "tensor", "fsdp"),
            P("replica", "tensor", "fsdp"),
            P("replica", "tensor", "fsdp"),
            P("replica", "tensor", "fsdp"),
        ),
        check_vma=False,
    )
```
